128 devices in a mesh: gx: 8 (over z, core), gy: 16 (over x, y).
Axes of the slice: x: 4, y: 4, z: 4, core: 2. Of those that a mesh axis runs over, the one named last changes fastest.
Arguments:
- tokens: bfloat16 [64, 14848], P(None, ('gy', 'gx'))
- lengths: int32 [64], P('gy'), may hold values from 1 to 4096, as said below
- gain_attn: float32 [14848], P('gy'), may hold values from 0.1 to 1.9
- bias_attn: float32 [14848], P('gy'), may hold values from -1.5 to 1.5
- gain_mlp: float32 [14848], P('gy'), may hold values from 0.1 to 1.9
- bias_mlp: float32 [14848], P('gy'), may hold values from -1.5 to 1.5
- w_qkv: bfloat16 [14848, 15872], P('gy', 'gx'), may hold values from -0.046875 to 0.046875
- w_out: bfloat16 [14848, 14848], P('gx', 'gy'), may hold values from -0.046875 to 0.046875
- w_up: bfloat16 [14848, 29696], P('gy', 'gx'), may hold values from -0.046875 to 0.046875
- w_down: bfloat16 [29696, 14848], P('gx', 'gy'), may hold values from -0.03125 to 0.03125
- cache: bfloat16 [64, 8, 4096, 128], P('gy', 'gx')
Outputs:
- mixed: bfloat16 [64, 14848], P(None, ('gy', 'gx'))
- new_kv: bfloat16 [64, 8, 128], P('gy', 'gx')
The draws below stay inside these ranges and needn't reach their ends.
Inputs may be any that keep to these rules, and one draw needn't show every extreme that they name: Row r's cache holds lengths[r] valid slots at its start; the slots after them hold values that must be ignored. Some row in every draw has all 4096 slots valid.
All inputs are finite; a program needn't handle non-finite values.
Results may differ from the reference program's by a relative error of at most 0.035.
Values may be sent and summed in bfloat16 or wider, within the bound.
No kernel may reach another device: no remote copies, remote signals or barrier semaphores. Data moves between devices by JAX's collectives and lax.ppermute only.
A program may use at most 128 MiB of HBM per device.

```python
import math
import jax
import jax.numpy as jnp
from jax import lax

D = 14848
HEADS = 232
KVH = 8
HD = 64
FF = 29696
ROWS = 64
LEN = 4096
QPG = 29
QKVW = 15872


def draw_tokens(key, part):
    key = jax.random.fold_in(key, 11)
    first = jax.random.fold_in(key, 0)
    column = jnp.arange(D, dtype=jnp.float32) / D
    noise = jax.random.normal(first, (ROWS, D), jnp.float32)
    drawn = noise * (0.6 * jnp.power(3.0, column))[None, :]
    return drawn.astype(jnp.bfloat16)


def draw_lengths(key, part):
    key = jax.random.fold_in(key, 12)
    first, second = jax.random.split(key)
    drawn = jax.random.randint(first, (ROWS,), 1, LEN + 1, dtype=jnp.int32)
    chosen = jax.random.randint(second, (), 0, ROWS, dtype=jnp.int32)
    return jnp.where(jnp.arange(ROWS, dtype=jnp.int32) == chosen, jnp.int32(LEN), drawn)


def draw_cache(key, part):
    key = jax.random.fold_in(key, 13)
    first = jax.random.fold_in(key, 0)
    fourth = jax.random.fold_in(key, 3)
    shape = (ROWS, KVH, LEN, HD)
    keys = jax.random.normal(first, shape, jnp.float32)
    values = jax.random.normal(fourth, shape, jnp.float32)
    return jnp.concatenate([keys, values], axis=-1).astype(jnp.bfloat16)


def block_levels(rng, dims, pieces, smallest, high):
    level, own = 1.0, jax.random.fold_in(rng, 6)
    for axis_at, blocks in pieces:
        draws = jnp.exp(jax.random.uniform(jax.random.fold_in(own, axis_at), (blocks,), jnp.float32, smallest / len(pieces), high / len(pieces)))
        level = level * jnp.repeat(draws, dims[axis_at] // blocks).reshape([-1 if axis == axis_at else 1 for axis in range(len(dims))])
    return level


def gaussian(rng, extent, spread, reach, shards=(), kind=jnp.bfloat16):
    level = block_levels(rng, extent, shards, -0.22, 0.18) if shards else 1.0
    values = jax.random.normal(rng, extent, jnp.float32) * spread * level
    return jnp.minimum(jnp.maximum(values, -reach), reach).astype(kind)


def setup_inputs(seed: int = 0) -> dict:
    seeds = jax.random.split(jax.random.key(seed), 12)
    tokens = draw_tokens(jax.random.fold_in(seeds[11], 71), 0)
    lengths = draw_lengths(jax.random.fold_in(seeds[11], 71), 0)
    gain_attn = jnp.clip(1.0 + 0.18 * jax.random.normal(seeds[2], (D,), jnp.float32), 0.1, 1.9)
    bias_attn = gaussian(seeds[3], (D,), 0.3, 1.5, ((0, 16),), jnp.float32)
    gain_mlp = jnp.clip(1.0 + 0.18 * jax.random.normal(seeds[4], (D,), jnp.float32), 0.1, 1.9)
    bias_mlp = gaussian(seeds[5], (D,), 0.3, 1.5, ((0, 16),), jnp.float32)
    w_qkv = gaussian(seeds[6], (D, QKVW), D ** -0.5, 0.046875, ((0, 16), (1, 8)))
    w_out = gaussian(seeds[7], (HEADS * HD, D), (HEADS * HD) ** -0.5, 0.046875, ((0, 8), (1, 16)))
    w_up = gaussian(seeds[8], (D, FF), D ** -0.5, 0.046875, ((0, 16), (1, 8)))
    w_down = gaussian(seeds[9], (FF, D), FF ** -0.5, 0.03125, ((0, 8), (1, 16)))
    cache = draw_cache(jax.random.fold_in(seeds[11], 71), 0)
    return dict(tokens=tokens, lengths=lengths, gain_attn=gain_attn, bias_attn=bias_attn, gain_mlp=gain_mlp, bias_mlp=bias_mlp, w_qkv=w_qkv, w_out=w_out, w_up=w_up, w_down=w_down, cache=cache)


EPS = 1e-05
THETA = 10000.0

def rotate(u, angle):
    half = u.shape[-1] // 2
    first = u[..., :half]
    second = u[..., half:]
    cosine = jnp.cos(angle)
    sine = jnp.sin(angle)
    return jnp.concatenate([first * cosine - second * sine, second * cosine + first * sine], axis=-1)

def angles(lengths, head_dim):
    steps = jnp.arange(head_dim // 2, dtype=jnp.float32) * (2.0 / head_dim)
    inverse = jnp.power(jnp.float32(THETA), -steps)
    return lengths.astype(jnp.float32)[:, None] * inverse[None, :]

def attend(query, key_new, value_new, cache, lengths):
    head_dim = query.shape[-1]
    scale = 1.0 / math.sqrt(head_dim)
    keys = cache[..., :head_dim].astype(jnp.float32)
    values = cache[..., head_dim:].astype(jnp.float32)
    query_f = query.astype(jnp.float32)
    scores = jnp.einsum('rgqd,rgtd->rgqt', query_f, keys) * scale
    positions = jnp.arange(cache.shape[2], dtype=jnp.int32)
    live = positions[None, None, None, :] < lengths.astype(jnp.int32)[:, None, None, None]
    scores = jnp.where(live, scores, -1e+30)
    own = jnp.einsum('rgqd,rgd->rgq', query_f, key_new.astype(jnp.float32)) * scale
    top = jnp.maximum(lax.optimization_barrier(jnp.max(scores, axis=-1)), own)
    probs = jnp.where(live, jnp.exp(scores - top[..., None]), 0.0)
    own_prob = jnp.exp(own - top)
    total = lax.optimization_barrier(jnp.sum(probs, axis=-1)) + own_prob
    weights = probs.astype(jnp.bfloat16).astype(jnp.float32)
    own_weight = own_prob.astype(jnp.bfloat16).astype(jnp.float32)
    summed = jnp.einsum('rgqt,rgtd->rgqd', weights, values)
    summed = summed + own_weight[..., None] * value_new.astype(jnp.float32)[:, :, None, :]
    result = (summed / total[..., None]).astype(jnp.bfloat16)
    return result.reshape(result.shape[0], -1)

def reference(tokens, lengths, gain_attn, bias_attn, gain_mlp, bias_mlp, w_qkv, w_out, w_up, w_down, cache):
    values = tokens.astype(jnp.float32)
    mean = lax.optimization_barrier(jnp.sum(values, axis=1)) / D
    var = lax.optimization_barrier(jnp.sum(values * values, axis=1)) / D - mean * mean
    centred = (values - mean[:, None]) / jnp.sqrt(var + EPS)[:, None]
    h_attn = (centred * gain_attn + bias_attn).astype(jnp.bfloat16)
    h_mlp = (centred * gain_mlp + bias_mlp).astype(jnp.bfloat16)
    qkv = jnp.dot(h_attn, w_qkv, preferred_element_type=jnp.float32).astype(jnp.bfloat16)
    qkv = qkv.reshape(ROWS, KVH, QPG + 2, HD)
    angle = angles(lengths, HD)
    query = rotate(qkv[:, :, :QPG].astype(jnp.float32), angle[:, None, None, :]).astype(jnp.bfloat16)
    key_new = rotate(qkv[:, :, QPG].astype(jnp.float32), angle[:, None, :]).astype(jnp.bfloat16)
    value_new = qkv[:, :, QPG + 1]
    new_kv = jnp.concatenate([key_new, value_new], axis=-1)

    def one_row(item):
        row_query, row_key, row_value, row_cache, row_length = item
        return attend(row_query[None], row_key[None], row_value[None], row_cache[None], row_length[None])[0]
    attn = lax.map(one_row, (query, key_new, value_new, cache, lengths))
    attn_part = jnp.dot(attn, w_out, preferred_element_type=jnp.float32)
    up = jnp.dot(h_mlp, w_up, preferred_element_type=jnp.float32)
    hidden = jax.nn.gelu(up, approximate=False).astype(jnp.bfloat16)
    mlp_part = jnp.dot(hidden, w_down, preferred_element_type=jnp.float32)
    mixed = (values + attn_part + mlp_part).astype(jnp.bfloat16)
    return (mixed, new_kv)
```

```python
import math

import jax
import jax.numpy as jnp
from jax import lax
from jax.sharding import PartitionSpec as P

HD = 64
QPG = 29
EPS = 1e-05
THETA = 10000.0
BF = jnp.bfloat16
F32 = jnp.float32


def rotate(u, angle):
    half = u.shape[-1] // 2
    first = u[..., :half]
    second = u[..., half:]
    cosine = jnp.cos(angle)
    sine = jnp.sin(angle)
    return jnp.concatenate(
        [first * cosine - second * sine, second * cosine + first * sine], axis=-1
    )


def angles(lengths, head_dim):
    steps = jnp.arange(head_dim // 2, dtype=F32) * (2.0 / head_dim)
    inverse = jnp.power(F32(THETA), -steps)
    return lengths.astype(F32)[:, None] * inverse[None, :]


def attend_local(query, key_new, value_new, cache, lengths):
    head_dim = query.shape[-1]
    scale = 1.0 / math.sqrt(head_dim)
    keys = cache[..., :head_dim]
    values = cache[..., head_dim:]
    scores = jnp.einsum("rgqd,rgtd->rgqt", query, keys, preferred_element_type=F32) * scale
    positions = jnp.arange(cache.shape[2], dtype=jnp.int32)
    live = positions[None, None, None, :] < lengths[:, None, None, None]
    scores = jnp.where(live, scores, -1e30)
    own = jnp.einsum("rgqd,rgd->rgq", query, key_new, preferred_element_type=F32) * scale
    top = jnp.maximum(jnp.max(scores, axis=-1), own)
    probs = jnp.where(live, jnp.exp(scores - top[..., None]), 0.0)
    own_prob = jnp.exp(own - top)
    total = jnp.sum(probs, axis=-1) + own_prob
    weights = probs.astype(BF)
    own_weight = own_prob.astype(BF).astype(F32)
    summed = jnp.einsum("rgqt,rgtd->rgqd", weights, values, preferred_element_type=F32)
    summed = summed + own_weight[..., None] * value_new.astype(F32)[:, :, None, :]
    result = (summed / total[..., None]).astype(BF)
    return result.reshape(result.shape[0], -1)


def pieces(value, count):
    out = []
    for _ in range(count):
        part = value.astype(BF)
        out.append(part)
        value = value - part.astype(F32)
    return out


def swap_core(x):
    return lax.ppermute(x, "gx", [(i, i ^ 1) for i in range(8)])


def shift_z(x, k):
    return lax.ppermute(x, "gx", [(i, (i + 2 * k) % 8) for i in range(8)])


def gather_tokens(tokens):
    core = lax.axis_index("gx") % 2
    z = lax.axis_index("gx") // 2
    other = swap_core(tokens)
    pair = jnp.stack([jnp.where(core == 0, tokens, other), jnp.where(core == 0, other, tokens)])
    got = [pair] + [shift_z(pair, k) for k in (1, 2, 3)]
    ring = jnp.stack([got[0], got[3], got[2], got[1]])
    ring = jnp.roll(ring, z, axis=0)
    return ring.reshape(8, *tokens.shape).transpose(1, 0, 2).reshape(tokens.shape[0], -1)


def local(
    tokens, lengths, gain_attn, bias_attn, gain_mlp, bias_mlp, w_qkv, w_out, w_up, w_down, cache
):
    rows = tokens.shape[0]
    size_gy = lax.axis_size("gy")
    own_rows = rows // size_gy
    wide = gain_attn.shape[0]
    width = wide * size_gy
    up_cols, qkv_cols = w_up.shape[1], w_qkv.shape[1]

    values = gather_tokens(tokens).astype(F32)
    part_sum = jnp.sum(values, axis=1)
    centre = part_sum / wide
    shifted = values - centre[:, None]
    part_square = jnp.sum(shifted * shifted, axis=1)

    def product(gain, bias, weight):
        left = jnp.concatenate(
            [
                (shifted * gain).astype(BF),
                jnp.stack(pieces(gain, 2) + pieces(bias, 2)),
            ]
        )
        out = jnp.dot(left, weight, preferred_element_type=F32)
        main = out[:rows].astype(BF).reshape(size_gy, own_rows, -1)
        vectors = jnp.stack(
            pieces(out[rows] + out[rows + 1], 2) + pieces(out[rows + 2] + out[rows + 3], 2)
        )
        vectors = jnp.broadcast_to(vectors[None], (size_gy,) + vectors.shape)
        return jnp.concatenate([main, vectors], axis=1)

    stats = jnp.stack(pieces(part_sum, 3) + pieces(part_square, 3), axis=-1)
    stats = stats.reshape(size_gy, own_rows, 6)
    stats = jnp.pad(stats, ((0, 0), (0, 4), (0, 58)))
    payload = jnp.concatenate(
        [product(gain_mlp, bias_mlp, w_up), product(gain_attn, bias_attn, w_qkv), stats], axis=2
    )
    got = lax.all_to_all(payload, "gy", 0, 0).astype(F32)

    stat = got[:, :own_rows, up_cols + qkv_cols :]
    sums = stat[..., 0] + stat[..., 1] + stat[..., 2]
    squares = stat[..., 3] + stat[..., 4] + stat[..., 5]
    mean = jnp.sum(sums, axis=0) / width
    gap = sums / wide - mean
    var = jnp.sum(squares + wide * gap * gap, axis=0) / width
    scale = 1.0 / jnp.sqrt(var + EPS)
    main = got[:, :own_rows, : up_cols + qkv_cols]
    gains = (got[:, 4] + got[:, 5])[:, None, : up_cols + qkv_cols]
    biases = (got[:, 6] + got[:, 7])[:, : up_cols + qkv_cols]
    full = scale[:, None] * jnp.sum(main + gap[..., None] * gains, axis=0) + jnp.sum(biases, axis=0)

    hidden = jax.nn.gelu(full[:, :up_cols], approximate=False).astype(BF)
    qkv = full[:, up_cols:].astype(BF).reshape(own_rows, 1, QPG + 2, HD)
    angle = angles(lengths, HD)
    query = rotate(qkv[:, :, :QPG].astype(F32), angle[:, None, None, :]).astype(BF)
    key_new = rotate(qkv[:, :, QPG].astype(F32), angle[:, None, :]).astype(BF)
    value_new = qkv[:, :, QPG + 1]
    new_kv = jnp.concatenate([key_new, value_new], axis=-1)
    attn = attend_local(query, key_new, value_new, cache, lengths)

    block = jnp.concatenate([hidden, attn], axis=1)
    block = jnp.broadcast_to(block[None], (size_gy,) + block.shape)
    every = lax.all_to_all(block, "gy", 0, 0).reshape(rows, -1)
    part = jnp.dot(every[:, :up_cols], w_down, preferred_element_type=F32) + jnp.dot(
        every[:, up_cols:], w_out, preferred_element_type=F32
    )

    core = lax.axis_index("gx") % 2
    z = lax.axis_index("gx") // 2
    blocks = part.reshape(rows, 4, 2, -1).transpose(2, 1, 0, 3)
    keep = jnp.where(core == 0, blocks[0], blocks[1])
    send = jnp.where(core == 0, blocks[1], blocks[0])
    keep = keep + swap_core(send)
    turned = jnp.roll(keep, -z, axis=0)
    narrow = turned.astype(BF)
    total = turned[0]
    for k in (1, 2, 3):
        total = total + shift_z(narrow[k], k).astype(F32)
    mixed = (tokens.astype(F32) + total).astype(BF)
    return (mixed, new_kv)


def solution(mesh):
    in_specs = (
        P(None, ("gy", "gx")),
        P("gy"),
        P("gy"),
        P("gy"),
        P("gy"),
        P("gy"),
        P("gy", "gx"),
        P("gx", "gy"),
        P("gy", "gx"),
        P("gx", "gy"),
        P("gy", "gx", None, None),
    )
    out_specs = (P(None, ("gy", "gx")), P("gy", "gx", None))
    return jax.shard_map(local, mesh=mesh, in_specs=in_specs, out_specs=out_specs, check_vma=False)
```

```python
import functools
import math

import jax
import jax.numpy as jnp
import numpy as np
from jax import lax
from jax.experimental import pallas as pl
from jax.experimental.pallas import tpu as pltpu
from jax.sharding import PartitionSpec as P

HD = 64
QPG = 29
EPS = 1e-05
THETA = 10000.0
BF = jnp.bfloat16
F32 = jnp.float32
LANES = 128
GY = 16
OWN = 4
ROWS = GY * OWN
BLOCK = 256
QKV_BLOCKS = 8
AT_SIDE = ROWS
AT_QKV = AT_SIDE + 8
AT_GAIN = AT_QKV + OWN * QKV_BLOCKS
AT_BIAS = AT_GAIN + QKV_BLOCKS
PAYLOAD = AT_BIAS + QKV_BLOCKS
RESULT = ROWS + OWN * QKV_BLOCKS
VM = pl.BlockSpec(memory_space=pltpu.VMEM)
SM = pl.BlockSpec(memory_space=pltpu.SMEM)
HB = pl.BlockSpec(memory_space=pl.ANY)
PARAMS = pltpu.CompilerParams(vmem_limit_bytes=16 << 20)


def in_vmem(x):
    return pltpu.with_memory_space_constraint(x, pltpu.VMEM)


def swap_core(x):
    return lax.ppermute(x, "gx", [(i, i ^ 1) for i in range(8)])


def shift_z(x, k):
    return lax.ppermute(x, "gx", [(i, (i + 2 * k) % 8) for i in range(8)])


def chunks(total, step):
    return [(at, min(step, total - at)) for at in range(0, total, step)]


def place():
    at = lax.axis_index("gx")
    return lax.div(at, 2), lax.rem(at, 2)


def three(value):
    out = []
    for _ in range(3):
        part = value.astype(BF).astype(F32)
        out.append(part)
        value = value - part
    return out


def product_kernel(g0, g1, g2, g3, gm, bm, ga, ba, w_up, w_qkv, out, blocks, flat, spread, side):
    z, core = place()
    narrow = g0.shape[2]
    wide = 8 * narrow
    for k, g in enumerate((g0, g1, g2, g3)):
        at = lax.rem(z + 4 - k, 4)
        blocks[2 * at + core] = g[0]
        blocks[2 * at + 1 - core] = g[1]
    for i in range(8):
        flat[:, narrow * i : narrow * (i + 1)] = blocks[i].astype(F32)
    values = flat[...]
    part_sum = jnp.sum(values, axis=1, keepdims=True)
    shifted = values - part_sum * (1.0 / wide)
    part_square = jnp.sum(shifted * shifted, axis=1, keepdims=True)
    up_cols, qkv_cols = w_up.shape[1], w_qkv.shape[1]

    lane = lax.broadcasted_iota(jnp.int32, (ROWS, LANES), 1)
    stats = jnp.zeros(lane.shape, F32)
    for i, part in enumerate(three(part_sum) + three(part_square)):
        stats = jnp.where(lane == 2 + i, part, stats)
    stats = jnp.transpose(stats)[:8]
    stats = jnp.concatenate([stats, jnp.zeros((8, BLOCK - ROWS), F32)], axis=1)
    row = lax.broadcasted_iota(jnp.int32, (8, 1), 0)

    def left(gain, bias):
        lower = jnp.where(row == 0, gain[...], jnp.where(row == 1, bias[...], 0.0))
        return jnp.concatenate([shifted * gain[...], lower], axis=0).astype(BF)

    left_m = left(gm, bm)
    for at, size in chunks(up_cols, 2 * BLOCK):
        got = jnp.dot(left_m, w_up[:, at : at + size], preferred_element_type=F32)
        if size < 2 * BLOCK:
            got = jnp.concatenate([got, jnp.zeros((ROWS + 8, 2 * BLOCK - size), F32)], axis=1)
        for j in range(2):
            p = at // BLOCK + j
            part = got[:, j * BLOCK : (j + 1) * BLOCK]
            out[p, :ROWS, :] = part[:ROWS].astype(BF)
            out[p, AT_SIDE:AT_QKV, :] = jnp.where(row < 2, part[ROWS:], stats).astype(BF)
    left_a = left(ga, ba)
    for at, size in chunks(qkv_cols, 2 * BLOCK):
        got = jnp.dot(left_a, w_qkv[:, at : at + size], preferred_element_type=F32)
        if size < 2 * BLOCK:
            got = jnp.concatenate([got, jnp.zeros((ROWS + 8, 2 * BLOCK - size), F32)], axis=1)
        for j in range(2):
            b = at // BLOCK + j
            part = got[:, j * BLOCK : (j + 1) * BLOCK]
            for h in range(2):
                cols = slice(h * LANES, (h + 1) * LANES)
                spread[h, pl.ds(b, ROWS, stride=QKV_BLOCKS), :] = part[:ROWS, cols]
            side[b : b + 1, :] = part[ROWS : ROWS + 1]
            side[QKV_BLOCKS + b : QKV_BLOCKS + b + 1, :] = part[ROWS + 1 : ROWS + 2]
    both = side[...].astype(BF)
    step = OWN * QKV_BLOCKS
    for p in range(GY):
        for h in range(2):
            cols = slice(h * LANES, (h + 1) * LANES)
            out[p, AT_QKV:AT_GAIN, cols] = spread[h, p * step : (p + 1) * step, :].astype(BF)
        out[p, AT_GAIN:, :] = both


def middle_kernel(wide, lengths, got, inverse, cache, block, new_kv, columns):
    width = wide * GY
    own_at = lax.axis_index("gy") * OWN

    sums, squares = [], []
    for d in range(GY):
        stat = got[d, AT_SIDE:AT_QKV, :LANES].astype(F32)
        sums.append(stat[2:3] + stat[3:4] + stat[4:5])
        squares.append(stat[5:6] + stat[6:7] + stat[7:8])
    mean = functools.reduce(jnp.add, sums) * (1.0 / width)
    gaps = [s * (1.0 / wide) - mean for s in sums]
    var = functools.reduce(jnp.add, [q + wide * g * g for q, g in zip(squares, gaps)]) * (1.0 / width)
    scale = 1.0 / jnp.sqrt(var + EPS)
    table = jnp.concatenate(gaps + [scale, jnp.zeros((LANES - GY - 1, LANES), F32)], axis=0)
    columns[...] = jnp.transpose(table)
    whole = columns[:ROWS]

    acc = jnp.zeros((ROWS, BLOCK), F32)
    plain = jnp.zeros((1, BLOCK), F32)
    for d in range(GY):
        side = got[d, AT_SIDE:AT_QKV, :].astype(F32)
        acc = acc + (got[d, :ROWS, :].astype(F32) + whole[:, d : d + 1] * side[0:1])
        plain = plain + side[1:2]
    up = whole[:, GY : GY + 1] * acc + plain
    hidden = 0.5 * up * (1.0 + lax.erf(up * math.sqrt(0.5)))
    block[:ROWS, :] = hidden.astype(BF)

    plain = jnp.zeros((QKV_BLOCKS, BLOCK), F32)
    for d in range(GY):
        plain = plain + got[d, AT_BIAS:, :].astype(F32)
    lane = lax.broadcasted_iota(jnp.int32, (1, LANES), 1)
    first = lane < HD
    half = lane % HD < HD // 2
    length = cache.shape[2]
    position = lax.broadcasted_iota(jnp.int32, (1, length), 1)
    factor = 1.0 / math.sqrt(HD)
    for r in range(OWN):
        mine = columns[pl.ds(own_at + r, 1), :]
        acc = jnp.zeros((QKV_BLOCKS, BLOCK), F32)
        for d in range(GY):
            lo = AT_QKV + QKV_BLOCKS * r
            part = got[d, lo : lo + QKV_BLOCKS, :].astype(F32)
            acc = acc + (part + mine[:, d : d + 1] * got[d, AT_GAIN:AT_BIAS, :].astype(F32))
        qkv = (mine[:, GY : GY + 1] * acc + plain).astype(BF).astype(F32)
        angle = lengths[r].astype(F32) * inverse[...]
        cosine = jnp.cos(angle)
        sine = jnp.sin(angle)
        sine = jnp.where(half, -sine, sine)
        pieces = []
        for h in range(2):
            pairs = qkv[:, h * LANES : (h + 1) * LANES]
            other = jnp.where(
                half, pltpu.roll(pairs, LANES - HD // 2, 1), pltpu.roll(pairs, HD // 2, 1)
            )
            turned = (pairs * cosine + other * sine).astype(BF).astype(F32)
            pieces.append(jnp.where(first, turned, 0.0))
            pieces.append(jnp.where(first, pltpu.roll(turned, HD, 1), 0.0))
        query = jnp.concatenate(pieces, axis=0)
        key = query[15:16]
        value = jnp.where(first, 0.0, pltpu.roll(qkv[7:8, LANES:], HD, 1))
        new_kv[r] = (key + value).astype(BF)
        keys = cache[r, 0]
        scores = lax.dot_general(
            query.astype(BF), keys, (((1,), (1,)), ((), ())), preferred_element_type=F32
        )
        scores = scores * factor
        live = position < lengths[r]
        scores = jnp.where(live, scores, -1e30)
        own = jnp.sum(query * key, axis=1, keepdims=True) * factor
        top = jnp.maximum(jnp.max(scores, axis=1, keepdims=True), own)
        probs = jnp.where(live, jnp.exp(scores - top), 0.0)
        own_prob = jnp.exp(own - top)
        total = jnp.sum(probs, axis=1, keepdims=True) + own_prob
        summed = jnp.dot(probs.astype(BF), keys, preferred_element_type=F32)
        summed = summed + own_prob.astype(BF).astype(F32) * value
        result = summed / total
        lo = ROWS + QKV_BLOCKS * r
        for h in range(2):
            even, odd = result[16 * h : 16 * h + 8], result[16 * h + 8 : 16 * h + 16]
            pairs = jnp.where(first, pltpu.roll(even, HD, 1), odd)
            block[lo : lo + QKV_BLOCKS, h * LANES : (h + 1) * LANES] = pairs.astype(BF)


def last_kernel(every, w_down, w_out, keep, send, spread, blocks):
    z, core = place()
    up_cols, attn_cols = w_down.shape[1], w_out.shape[1]
    narrow = keep.shape[2]
    both = (((1,), (1,)), ((), ()))
    step = OWN * QKV_BLOCKS
    for d in range(GY):
        for h in range(2):
            cols = slice(h * LANES, (h + 1) * LANES)
            spread[h, d * step : (d + 1) * step, :] = every[d, ROWS:, cols].astype(F32)
    part = jnp.zeros((ROWS, w_down.shape[0]), F32)
    for d, (at, size) in enumerate(chunks(up_cols, BLOCK)):
        part = part + lax.dot_general(
            every[d, :ROWS, :size], w_down[:, at : at + size], both, preferred_element_type=F32
        )
    for b, (at, size) in enumerate(chunks(attn_cols, BLOCK)):
        left = [spread[h, pl.ds(b, ROWS, stride=QKV_BLOCKS), :].astype(BF) for h in range(2)]
        left = jnp.concatenate(left, axis=1)
        part = part + lax.dot_general(
            left[:, :size], w_out[:, at : at + size], both, preferred_element_type=F32
        )
    for i in range(8):
        blocks[i] = part[:, narrow * i : narrow * (i + 1)]
    for k in range(4):
        at = lax.rem(z + k, 4)
        keep[k] = blocks[2 * at + core]
        send[k] = blocks[2 * at + 1 - core]


def local(
    tokens, lengths, gain_attn, bias_attn, gain_mlp, bias_mlp, w_qkv, w_out, w_up, w_down, cache
):
    rows, narrow = tokens.shape
    wide = gain_attn.shape[0]

    pair = jnp.stack([tokens, swap_core(tokens)])
    got = [pair] + [shift_z(pair, k) for k in (1, 2, 3)]
    vectors = [v.reshape(1, wide) for v in (gain_mlp, bias_mlp, gain_attn, bias_attn)]
    payload = pl.pallas_call(
        product_kernel,
        out_shape=jax.ShapeDtypeStruct((GY, PAYLOAD, BLOCK), BF),
        in_specs=[VM] * 10,
        out_specs=VM,
        scratch_shapes=[
            pltpu.VMEM((8, rows, narrow), BF),
            pltpu.VMEM((rows, wide), F32),
            pltpu.VMEM((2, rows * QKV_BLOCKS, LANES), F32),
            pltpu.VMEM((2 * QKV_BLOCKS, BLOCK), F32),
        ],
        compiler_params=PARAMS,
        name="product",
    )(*got, *vectors, in_vmem(w_up), in_vmem(w_qkv))

    steps = np.arange(HD // 2, dtype=np.float64) * (2.0 / HD)
    inverse = jnp.asarray(np.tile(np.power(THETA, -steps), 4)[None].astype(np.float32))
    summed = lax.all_to_all(payload, "gy", 0, 0)
    block, new_kv = pl.pallas_call(
        functools.partial(middle_kernel, wide),
        out_shape=(
            jax.ShapeDtypeStruct((RESULT, BLOCK), BF),
            jax.ShapeDtypeStruct((OWN, 1, 2 * HD), BF),
        ),
        in_specs=[SM] + [VM] * 3,
        out_specs=(VM, VM),
        scratch_shapes=[pltpu.VMEM((LANES, LANES), F32)],
        compiler_params=PARAMS,
        name="middle",
    )(lengths, summed, inverse, in_vmem(cache))

    every = lax.all_to_all(jnp.broadcast_to(block[None], (GY, RESULT, BLOCK)), "gy", 0, 0)
    half = jax.ShapeDtypeStruct((4, rows, narrow), F32)
    keep, send = pl.pallas_call(
        last_kernel,
        out_shape=(half, half),
        in_specs=[VM] * 3,
        out_specs=(VM, VM),
        scratch_shapes=[
            pltpu.VMEM((2, rows * QKV_BLOCKS, LANES), F32),
            pltpu.VMEM((8, rows, narrow), F32),
        ],
        compiler_params=PARAMS,
        name="last",
    )(every, in_vmem(w_down.T), in_vmem(w_out.T))

    keep = keep + swap_core(send)
    narrowed = keep.astype(BF)
    total = keep[0]
    for k in (1, 2, 3):
        total = total + shift_z(narrowed[k], k).astype(F32)
    mixed = (tokens.astype(F32) + total).astype(BF)
    return (mixed, new_kv)


def solution(mesh):
    in_specs = (
        P(None, ("gy", "gx")),
        P("gy"),
        P("gy"),
        P("gy"),
        P("gy"),
        P("gy"),
        P("gy", "gx"),
        P("gx", "gy"),
        P("gy", "gx"),
        P("gx", "gy"),
        P("gy", "gx", None, None),
    )
    out_specs = (P(None, ("gy", "gx")), P("gy", "gx", None))
    return jax.shard_map(local, mesh=mesh, in_specs=in_specs, out_specs=out_specs, check_vma=False)
```

```python
import functools
import math

import jax
import jax.numpy as jnp
import numpy as np
from jax import lax
from jax.experimental import pallas as pl
from jax.experimental.pallas import tpu as pltpu
from jax.sharding import PartitionSpec as P

HD = 64
QPG = 29
EPS = 1e-05
THETA = 10000.0
BF = jnp.bfloat16
F32 = jnp.float32
LANES = 128
GY = 16
OWN = 4
ROWS = GY * OWN
BLOCK = 256
QKV_BLOCKS = 8
AT_SIDE = ROWS
AT_QKV = AT_SIDE + 8
AT_GAIN = AT_QKV + OWN * QKV_BLOCKS
AT_BIAS = AT_GAIN + QKV_BLOCKS
PAYLOAD = AT_BIAS + QKV_BLOCKS
RESULT = ROWS + OWN * QKV_BLOCKS
VM = pl.BlockSpec(memory_space=pltpu.VMEM)
SM = pl.BlockSpec(memory_space=pltpu.SMEM)
PARAMS = pltpu.CompilerParams(vmem_limit_bytes=16 << 20)


def in_vmem(x):
    return pltpu.with_memory_space_constraint(x, pltpu.VMEM)


def hold_kernel(mine, out, sem):
    copy = pltpu.make_async_copy(mine, out, sem)
    copy.start()
    copy.wait()


def pair_kernel(mine, other, out):
    out[0] = mine[...]
    out[1] = other[...]


def swap_core(x):
    return lax.ppermute(x, "gx", [(i, i ^ 1) for i in range(8)])


def shift_z(x, k):
    return lax.ppermute(x, "gx", [(i, (i + 2 * k) % 8) for i in range(8)])


def chunks(total, step):
    return [(at, min(step, total - at)) for at in range(0, total, step)]


def three(value):
    out = []
    for _ in range(3):
        part = value.astype(BF).astype(F32)
        out.append(part)
        value = value - part
    return out


def product_kernel(g0, g1, g2, g3, gm, bm, ga, ba, w_up, w_qkv, out, blocks, flat, spread, side):
    at = lax.axis_index("gx")
    z, core = lax.div(at, 2), lax.rem(at, 2)
    narrow = g0.shape[2]
    wide = 8 * narrow
    for k, g in enumerate((g0, g1, g2, g3)):
        at = lax.rem(z + 4 - k, 4)
        blocks[2 * at + core] = g[0]
        blocks[2 * at + 1 - core] = g[1]
    for i in range(8):
        flat[:, narrow * i : narrow * (i + 1)] = blocks[i].astype(F32)
    values = flat[...]
    part_sum = jnp.sum(values, axis=1, keepdims=True)
    shifted = values - part_sum * (1.0 / wide)
    part_square = jnp.sum(shifted * shifted, axis=1, keepdims=True)
    up_cols, qkv_cols = w_up.shape[1], w_qkv.shape[1]

    lane = lax.broadcasted_iota(jnp.int32, (ROWS, LANES), 1)
    stats = jnp.zeros(lane.shape, F32)
    for i, part in enumerate(three(part_sum) + three(part_square)):
        stats = jnp.where(lane == 2 + i, part, stats)
    stats = jnp.transpose(stats)[:8]
    stats = jnp.concatenate([stats, jnp.zeros((8, BLOCK - ROWS), F32)], axis=1)
    row = lax.broadcasted_iota(jnp.int32, (8, 1), 0)

    def left(gain, bias):
        lower = jnp.where(row == 0, gain[...], jnp.where(row == 1, bias[...], 0.0))
        return jnp.concatenate([shifted * gain[...], lower], axis=0).astype(BF)

    left_m = left(gm, bm)
    for at, size in chunks(up_cols, 2 * BLOCK):
        got = jnp.dot(left_m, w_up[:, at : at + size], preferred_element_type=F32)
        if size < 2 * BLOCK:
            got = jnp.concatenate([got, jnp.zeros((ROWS + 8, 2 * BLOCK - size), F32)], axis=1)
        for j in range(2):
            p = at // BLOCK + j
            part = got[:, j * BLOCK : (j + 1) * BLOCK]
            out[p, :ROWS, :] = part[:ROWS].astype(BF)
            out[p, AT_SIDE:AT_QKV, :] = jnp.where(row < 2, part[ROWS:], stats).astype(BF)
    left_a = left(ga, ba)
    for at, size in chunks(qkv_cols, 2 * BLOCK):
        got = jnp.dot(left_a, w_qkv[:, at : at + size], preferred_element_type=F32)
        if size < 2 * BLOCK:
            got = jnp.concatenate([got, jnp.zeros((ROWS + 8, 2 * BLOCK - size), F32)], axis=1)
        for j in range(2):
            b = at // BLOCK + j
            part = got[:, j * BLOCK : (j + 1) * BLOCK]
            for h in range(2):
                cols = slice(h * LANES, (h + 1) * LANES)
                spread[h, pl.ds(b, ROWS, stride=QKV_BLOCKS), :] = part[:ROWS, cols]
            side[b : b + 1, :] = part[ROWS : ROWS + 1]
            side[QKV_BLOCKS + b : QKV_BLOCKS + b + 1, :] = part[ROWS + 1 : ROWS + 2]
    both = side[...].astype(BF)
    step = OWN * QKV_BLOCKS
    for p in range(GY):
        for h in range(2):
            cols = slice(h * LANES, (h + 1) * LANES)
            out[p, AT_QKV:AT_GAIN, cols] = spread[h, p * step : (p + 1) * step, :].astype(BF)
        out[p, AT_GAIN:, :] = both


def middle_kernel(wide, lengths, got, inverse, cache, block, new_kv, columns):
    width = wide * GY
    own_at = lax.axis_index("gy") * OWN

    sums, squares = [], []
    for d in range(GY):
        stat = got[d, AT_SIDE:AT_QKV, :LANES].astype(F32)
        sums.append(stat[2:3] + stat[3:4] + stat[4:5])
        squares.append(stat[5:6] + stat[6:7] + stat[7:8])
    mean = functools.reduce(jnp.add, sums) * (1.0 / width)
    gaps = [s * (1.0 / wide) - mean for s in sums]
    var = functools.reduce(jnp.add, [q + wide * g * g for q, g in zip(squares, gaps)]) * (1.0 / width)
    scale = 1.0 / jnp.sqrt(var + EPS)
    table = jnp.concatenate(gaps + [scale, jnp.zeros((LANES - GY - 1, LANES), F32)], axis=0)
    columns[...] = jnp.transpose(table)
    whole = columns[:ROWS]

    acc = jnp.zeros((ROWS, BLOCK), F32)
    plain = jnp.zeros((1, BLOCK), F32)
    for d in range(GY):
        side = got[d, AT_SIDE:AT_QKV, :].astype(F32)
        acc = acc + (got[d, :ROWS, :].astype(F32) + whole[:, d : d + 1] * side[0:1])
        plain = plain + side[1:2]
    up = whole[:, GY : GY + 1] * acc + plain
    hidden = 0.5 * up * (1.0 + lax.erf(up * math.sqrt(0.5)))
    block[:ROWS, :] = hidden.astype(BF)

    plain = jnp.zeros((QKV_BLOCKS, BLOCK), F32)
    for d in range(GY):
        plain = plain + got[d, AT_BIAS:, :].astype(F32)
    lane = lax.broadcasted_iota(jnp.int32, (1, LANES), 1)
    first = lane < HD
    half = lane % HD < HD // 2
    length = cache.shape[2]
    position = lax.broadcasted_iota(jnp.int32, (1, length), 1)
    factor = 1.0 / math.sqrt(HD)
    for r in range(OWN):
        mine = columns[pl.ds(own_at + r, 1), :]
        acc = jnp.zeros((QKV_BLOCKS, BLOCK), F32)
        for d in range(GY):
            lo = AT_QKV + QKV_BLOCKS * r
            part = got[d, lo : lo + QKV_BLOCKS, :].astype(F32)
            acc = acc + (part + mine[:, d : d + 1] * got[d, AT_GAIN:AT_BIAS, :].astype(F32))
        qkv = (mine[:, GY : GY + 1] * acc + plain).astype(BF).astype(F32)
        angle = lengths[r].astype(F32) * inverse[...]
        cosine = jnp.cos(angle)
        sine = jnp.sin(angle)
        sine = jnp.where(half, -sine, sine)
        pieces = []
        for h in range(2):
            pairs = qkv[:, h * LANES : (h + 1) * LANES]
            other = jnp.where(
                half, pltpu.roll(pairs, LANES - HD // 2, 1), pltpu.roll(pairs, HD // 2, 1)
            )
            turned = (pairs * cosine + other * sine).astype(BF).astype(F32)
            pieces.append(jnp.where(first, turned, 0.0))
            pieces.append(jnp.where(first, pltpu.roll(turned, HD, 1), 0.0))
        query = jnp.concatenate(pieces, axis=0)
        key = query[15:16]
        query = query * factor
        value = jnp.where(first, 0.0, pltpu.roll(qkv[7:8, LANES:], HD, 1))
        new_kv[r : r + 1, :] = (key + value).astype(BF)
        keys = cache[r, 0]
        scores = lax.dot_general(
            query.astype(BF), keys, (((1,), (1,)), ((), ())), preferred_element_type=F32
        )
        scores = jnp.where(position < lengths[r], scores, -jnp.inf)
        own = jnp.sum(query * key, axis=1, keepdims=True)
        top = jnp.maximum(jnp.max(scores, axis=1, keepdims=True), own)
        probs = jnp.exp(scores - top)
        own_prob = jnp.exp(own - top)
        total = jnp.sum(probs, axis=1, keepdims=True) + own_prob
        summed = jnp.dot(probs.astype(BF), keys, preferred_element_type=F32)
        summed = summed + own_prob.astype(BF).astype(F32) * value
        result = summed / total
        lo = ROWS + QKV_BLOCKS * r
        for h in range(2):
            even, odd = result[16 * h : 16 * h + 8], result[16 * h + 8 : 16 * h + 16]
            pairs = jnp.where(first, pltpu.roll(even, HD, 1), odd)
            block[lo : lo + QKV_BLOCKS, h * LANES : (h + 1) * LANES] = pairs.astype(BF)


def last_kernel(every, w_down, w_out, out, spread):
    up_cols, attn_cols = w_down.shape[1], w_out.shape[1]
    narrow = out.shape[2]
    both = (((1,), (1,)), ((), ()))
    step = OWN * QKV_BLOCKS
    for d in range(GY):
        for h in range(2):
            cols = slice(h * LANES, (h + 1) * LANES)
            spread[h, d * step : (d + 1) * step, :] = every[d, ROWS:, cols].astype(F32)
    part = jnp.zeros((ROWS, w_down.shape[0]), F32)
    for d, (at, size) in enumerate(chunks(up_cols, BLOCK)):
        part = part + lax.dot_general(
            every[d, :ROWS, :size], w_down[:, at : at + size], both, preferred_element_type=F32
        )
    for b, (at, size) in enumerate(chunks(attn_cols, BLOCK)):
        left = [spread[h, pl.ds(b, ROWS, stride=QKV_BLOCKS), :].astype(BF) for h in range(2)]
        left = jnp.concatenate(left, axis=1)
        part = part + lax.dot_general(
            left[:, :size], w_out[:, at : at + size], both, preferred_element_type=F32
        )
    for i in range(8):
        out[i] = part[:, narrow * i : narrow * (i + 1)].astype(BF)


def local(
    tokens, lengths, gain_attn, bias_attn, gain_mlp, bias_mlp, w_qkv, w_out, w_up, w_down, cache
):
    rows, narrow = tokens.shape
    wide = gain_attn.shape[0]

    mine = pl.pallas_call(
        hold_kernel,
        out_shape=pltpu.VMEM((rows, narrow), BF),
        in_specs=[pl.BlockSpec(memory_space=pl.ANY)],
        out_specs=VM,
        scratch_shapes=[pltpu.SemaphoreType.DMA],
        compiler_params=pltpu.CompilerParams(vmem_limit_bytes=1 << 20),
        cost_estimate=pl.CostEstimate(flops=20 << 30, bytes_accessed=96 << 20, transcendentals=0),
        name="hold",
    )(pltpu.with_memory_space_constraint(tokens, pltpu.HBM))
    pair = pl.pallas_call(
        pair_kernel,
        out_shape=jax.ShapeDtypeStruct((2, rows, narrow), BF),
        in_specs=[VM] * 2,
        out_specs=VM,
        compiler_params=pltpu.CompilerParams(vmem_limit_bytes=1 << 20),
        name="pair",
    )(in_vmem(mine), swap_core(tokens))
    got = [pair] + [shift_z(pair, k) for k in (1, 2, 3)]
    vectors = [v.reshape(1, wide) for v in (gain_mlp, bias_mlp, gain_attn, bias_attn)]
    held = vectors + [w_up, w_qkv]
    payload = pl.pallas_call(
        product_kernel,
        out_shape=jax.ShapeDtypeStruct((GY, PAYLOAD, BLOCK), BF),
        in_specs=[VM] * 10,
        out_specs=VM,
        scratch_shapes=[
            pltpu.VMEM((8, rows, narrow), BF),
            pltpu.VMEM((rows, wide), F32),
            pltpu.VMEM((2, rows * QKV_BLOCKS, LANES), F32),
            pltpu.VMEM((2 * QKV_BLOCKS, BLOCK), F32),
        ],
        compiler_params=PARAMS,
        name="product",
    )(*got, *[in_vmem(x) for x in held])

    steps = np.arange(HD // 2, dtype=np.float64) * (2.0 / HD)
    inverse = jnp.asarray(np.tile(np.power(THETA, -steps), 4)[None].astype(np.float32))
    summed = lax.all_to_all(payload, "gy", 0, 0)
    block, new_kv = pl.pallas_call(
        functools.partial(middle_kernel, wide),
        out_shape=(
            jax.ShapeDtypeStruct((RESULT, BLOCK), BF),
            jax.ShapeDtypeStruct((OWN, 2 * HD), BF),
        ),
        in_specs=[SM] + [VM] * 3,
        out_specs=(VM, VM),
        scratch_shapes=[pltpu.VMEM((LANES, LANES), F32)],
        compiler_params=PARAMS,
        name="middle",
    )(lengths, summed, inverse, in_vmem(cache))

    every = lax.all_to_all(jnp.broadcast_to(block[None], (GY, RESULT, BLOCK)), "gy", 0, 0)
    shares = pl.pallas_call(
        last_kernel,
        out_shape=jax.ShapeDtypeStruct((8, rows, narrow), BF),
        in_specs=[VM] * 3,
        out_specs=VM,
        scratch_shapes=[pltpu.VMEM((2, rows * QKV_BLOCKS, LANES), F32)],
        compiler_params=PARAMS,
        name="last",
    )(every, in_vmem(w_down.T), in_vmem(w_out.T))

    merged = jnp.sum(lax.all_to_all(shares, "gx", 0, 0).astype(F32), axis=0)
    mixed = (tokens.astype(F32) + merged).astype(BF)
    return (mixed, new_kv.reshape(OWN, 1, 2 * HD))


def solution(mesh):
    in_specs = (
        P(None, ("gy", "gx")),
        P("gy"),
        P("gy"),
        P("gy"),
        P("gy"),
        P("gy"),
        P("gy", "gx"),
        P("gx", "gy"),
        P("gy", "gx"),
        P("gx", "gy"),
        P("gy", "gx", None, None),
    )
    out_specs = (P(None, ("gy", "gx")), P("gy", "gx", None))
    return jax.shard_map(local, mesh=mesh, in_specs=in_specs, out_specs=out_specs, check_vma=False)
```

```python
import functools
import math

import jax
import jax.numpy as jnp
import numpy as np
from jax import lax
from jax.experimental import pallas as pl
from jax.experimental.pallas import tpu as pltpu
from jax.sharding import PartitionSpec as P

HD = 64
QPG = 29
EPS = 1e-05
THETA = 10000.0
BF = jnp.bfloat16
F32 = jnp.float32
LANES = 128
GY = 16
OWN = 4
ROWS = GY * OWN
BLOCK = 256
QKV_BLOCKS = 8
AT_SIDE = ROWS
AT_QKV = AT_SIDE + 8
AT_GAIN = AT_QKV + OWN * QKV_BLOCKS
AT_BIAS = AT_GAIN + QKV_BLOCKS
PAYLOAD = AT_BIAS + QKV_BLOCKS
RESULT = ROWS + OWN * QKV_BLOCKS
VM = pl.BlockSpec(memory_space=pltpu.VMEM)
SM = pl.BlockSpec(memory_space=pltpu.SMEM)
PARAMS = pltpu.CompilerParams(vmem_limit_bytes=16 << 20)


def in_vmem(x):
    return pltpu.with_memory_space_constraint(x, pltpu.VMEM)


def hold_kernel(mine, out, sem):
    copy = pltpu.make_async_copy(mine, out, sem)
    copy.start()
    copy.wait()


def pair_kernel(mine, other, out):
    out[0] = mine[...]
    out[1] = other[...]


def swap_core(x):
    return lax.ppermute(x, "gx", [(i, i ^ 1) for i in range(8)])


def shift_z(x, k):
    return lax.ppermute(x, "gx", [(i, (i + 2 * k) % 8) for i in range(8)])


def chunks(total, step):
    return [(at, min(step, total - at)) for at in range(0, total, step)]


def three(value):
    out = []
    for _ in range(3):
        part = value.astype(BF).astype(F32)
        out.append(part)
        value = value - part
    return out


def product_kernel(g0, g1, g2, g3, gm, bm, ga, ba, w_up, w_qkv, out, blocks, flat, spread, side):
    at = lax.axis_index("gx")
    z, core = lax.div(at, 2), lax.rem(at, 2)
    narrow = g0.shape[2]
    wide = 8 * narrow
    for k, g in enumerate((g0, g1, g2, g3)):
        at = lax.rem(z + 4 - k, 4)
        blocks[2 * at + core] = g[0]
        blocks[2 * at + 1 - core] = g[1]
    for i in range(8):
        flat[:, narrow * i : narrow * (i + 1)] = blocks[i].astype(F32)
    values = flat[...]
    part_sum = jnp.sum(values, axis=1, keepdims=True)
    shifted = values - part_sum * (1.0 / wide)
    part_square = jnp.sum(shifted * shifted, axis=1, keepdims=True)
    up_cols, qkv_cols = w_up.shape[1], w_qkv.shape[1]

    lane = lax.broadcasted_iota(jnp.int32, (ROWS, LANES), 1)
    stats = jnp.zeros(lane.shape, F32)
    for i, part in enumerate(three(part_sum) + three(part_square)):
        stats = jnp.where(lane == 2 + i, part, stats)
    stats = jnp.transpose(stats)[:8]
    stats = jnp.concatenate([stats, jnp.zeros((8, BLOCK - ROWS), F32)], axis=1)
    row = lax.broadcasted_iota(jnp.int32, (8, 1), 0)

    def left(gain, bias):
        lower = jnp.where(row == 0, gain[...], jnp.where(row == 1, bias[...], 0.0))
        return jnp.concatenate([shifted * gain[...], lower], axis=0).astype(BF)

    left_m = left(gm, bm)
    for at, size in chunks(up_cols, 2 * BLOCK):
        got = jnp.dot(left_m, w_up[:, at : at + size], preferred_element_type=F32)
        if size < 2 * BLOCK:
            got = jnp.concatenate([got, jnp.zeros((ROWS + 8, 2 * BLOCK - size), F32)], axis=1)
        for j in range(2):
            p = at // BLOCK + j
            part = got[:, j * BLOCK : (j + 1) * BLOCK]
            out[p, :ROWS, :] = part[:ROWS].astype(BF)
            out[p, AT_SIDE:AT_QKV, :] = jnp.where(row < 2, part[ROWS:], stats).astype(BF)
    left_a = left(ga, ba)
    for at, size in chunks(qkv_cols, 2 * BLOCK):
        got = jnp.dot(left_a, w_qkv[:, at : at + size], preferred_element_type=F32)
        if size < 2 * BLOCK:
            got = jnp.concatenate([got, jnp.zeros((ROWS + 8, 2 * BLOCK - size), F32)], axis=1)
        for j in range(2):
            b = at // BLOCK + j
            part = got[:, j * BLOCK : (j + 1) * BLOCK]
            for h in range(2):
                cols = slice(h * LANES, (h + 1) * LANES)
                spread[h, pl.ds(b, ROWS, stride=QKV_BLOCKS), :] = part[:ROWS, cols]
            side[b : b + 1, :] = part[ROWS : ROWS + 1]
            side[QKV_BLOCKS + b : QKV_BLOCKS + b + 1, :] = part[ROWS + 1 : ROWS + 2]
    both = side[...].astype(BF)
    step = OWN * QKV_BLOCKS
    for p in range(GY):
        for h in range(2):
            cols = slice(h * LANES, (h + 1) * LANES)
            out[p, AT_QKV:AT_GAIN, cols] = spread[h, p * step : (p + 1) * step, :].astype(BF)
        out[p, AT_GAIN:, :] = both


def middle_kernel(wide, lengths, got, inverse, cache, block, new_kv, columns):
    width = wide * GY
    own_at = lax.axis_index("gy") * OWN

    sums, squares = [], []
    for d in range(GY):
        stat = got[d, AT_SIDE:AT_QKV, :LANES].astype(F32)
        sums.append(stat[2:3] + stat[3:4] + stat[4:5])
        squares.append(stat[5:6] + stat[6:7] + stat[7:8])
    mean = functools.reduce(jnp.add, sums) * (1.0 / width)
    gaps = [s * (1.0 / wide) - mean for s in sums]
    var = functools.reduce(jnp.add, [q + wide * g * g for q, g in zip(squares, gaps)]) * (1.0 / width)
    scale = 1.0 / jnp.sqrt(var + EPS)
    table = jnp.concatenate(gaps + [scale, jnp.zeros((LANES - GY - 1, LANES), F32)], axis=0)
    columns[...] = jnp.transpose(table)
    whole = columns[:ROWS]

    plain = jnp.zeros((QKV_BLOCKS, BLOCK), F32)
    for d in range(GY):
        plain = plain + got[d, AT_BIAS:, :].astype(F32)
    lane = lax.broadcasted_iota(jnp.int32, (1, LANES), 1)
    first = lane < HD
    half = lane % HD < HD // 2
    length = cache.shape[2]
    position = lax.broadcasted_iota(jnp.int32, (1, length), 1)
    factor = 1.0 / math.sqrt(HD)

    queries, keys_new, values_new = [], [], []
    for r in range(OWN):
        mine = columns[pl.ds(own_at + r, 1), :]
        acc = jnp.zeros((QKV_BLOCKS, BLOCK), F32)
        for d in range(GY):
            lo = AT_QKV + QKV_BLOCKS * r
            part = got[d, lo : lo + QKV_BLOCKS, :].astype(F32)
            acc = acc + (part + mine[:, d : d + 1] * got[d, AT_GAIN:AT_BIAS, :].astype(F32))
        qkv = (mine[:, GY : GY + 1] * acc + plain).astype(BF).astype(F32)
        angle = lengths[r].astype(F32) * inverse[...]
        cosine = jnp.cos(angle)
        sine = jnp.sin(angle)
        sine = jnp.where(half, -sine, sine)
        pieces = []
        for h in range(2):
            pairs = qkv[:, h * LANES : (h + 1) * LANES]
            other = jnp.where(
                half, pltpu.roll(pairs, LANES - HD // 2, 1), pltpu.roll(pairs, HD // 2, 1)
            )
            turned = (pairs * cosine + other * sine).astype(BF).astype(F32)
            pieces.append(jnp.where(first, turned, 0.0))
            pieces.append(jnp.where(first, pltpu.roll(turned, HD, 1), 0.0))
        query = jnp.concatenate(pieces, axis=0)
        key = query[15:16]
        value = jnp.where(first, 0.0, pltpu.roll(qkv[7:8, LANES:], HD, 1))
        new_kv[r : r + 1, :] = (key + value).astype(BF)
        queries.append(query * factor)
        keys_new.append(key)
        values_new.append(value)

    def score(r):
        scores = lax.dot_general(
            queries[r].astype(BF), cache[r, 0], (((1,), (1,)), ((), ())), preferred_element_type=F32
        )
        return jnp.where(position < lengths[r], scores, -jnp.inf)

    def soften(r, scores):
        own = jnp.sum(queries[r] * keys_new[r], axis=1, keepdims=True)
        top = jnp.maximum(jnp.max(scores, axis=1, keepdims=True), own)
        probs = jnp.exp(scores - top)
        own_prob = jnp.exp(own - top)
        total = jnp.sum(probs, axis=1, keepdims=True) + own_prob
        return probs.astype(BF), own_prob, total

    def mix(r, probs, own_prob, total):
        summed = jnp.dot(probs, cache[r, 0], preferred_element_type=F32)
        summed = summed + own_prob.astype(BF).astype(F32) * values_new[r]
        result = summed / total
        lo = ROWS + QKV_BLOCKS * r
        for h in range(2):
            even, odd = result[16 * h : 16 * h + 8], result[16 * h + 8 : 16 * h + 16]
            pairs = jnp.where(first, pltpu.roll(even, HD, 1), odd)
            block[lo : lo + QKV_BLOCKS, h * LANES : (h + 1) * LANES] = pairs.astype(BF)

    soft = {}
    scores = score(0)
    for r in range(OWN):
        following = score(r + 1) if r + 1 < OWN else None
        soft[r] = soften(r, scores)
        if r > 0:
            mix(r - 1, *soft.pop(r - 1))
        scores = following

    acc = jnp.zeros((ROWS, BLOCK), F32)
    plain = jnp.zeros((1, BLOCK), F32)
    for d in range(GY):
        side = got[d, AT_SIDE:AT_QKV, :].astype(F32)
        acc = acc + (got[d, :ROWS, :].astype(F32) + whole[:, d : d + 1] * side[0:1])
        plain = plain + side[1:2]
    up = whole[:, GY : GY + 1] * acc + plain
    hidden = 0.5 * up * (1.0 + lax.erf(up * math.sqrt(0.5)))
    block[:ROWS, :] = hidden.astype(BF)
    mix(OWN - 1, *soft.pop(OWN - 1))


def last_kernel(every, w_down, w_out, out, spread, left, turned):
    up_cols, attn_cols = w_down.shape[1], w_out.shape[1]
    narrow = w_down.shape[0] // 8
    step = OWN * QKV_BLOCKS
    for d in range(GY):
        for h in range(2):
            cols = slice(h * LANES, (h + 1) * LANES)
            spread[h, d * step : (d + 1) * step, :] = every[d, ROWS:, cols].astype(F32)
    for d, (at, size) in enumerate(chunks(up_cols, BLOCK)):
        part = every[d, :ROWS, :size]
        left[:ROWS, at : at + size] = part
        left[ROWS:, at : at + size] = part
    for t in range(-(-attn_cols // LANES)):
        part = spread[t % 2, pl.ds(t // 2, ROWS, stride=QKV_BLOCKS), :].astype(BF)
        at = up_cols + t * LANES
        left[:ROWS, at : at + LANES] = part
        left[ROWS:, at : at + LANES] = part
    both = (((1,), (1,)), ((), ()))
    total = lax.dot_general(w_down[...], left[:, :up_cols], both, preferred_element_type=F32)
    total = total + lax.dot_general(
        w_out[...], left[:, up_cols : up_cols + attn_cols], both, preferred_element_type=F32
    )
    turned[: 8 * narrow, :] = total
    turned[8 * narrow :, :] = jnp.zeros((turned.shape[0] - 8 * narrow, LANES), F32)
    first = lax.broadcasted_iota(jnp.int32, (1, LANES), 1) < ROWS
    for i in range(8):
        at = narrow * i
        upper, lower = turned[at : at + ROWS, :], turned[at + ROWS : at + 2 * ROWS, :]
        out[i] = jnp.where(first, upper, lower).astype(BF)


def finish_kernel(shares, tokens, mixed):
    total = shares[0].astype(F32)
    for i in range(1, 8):
        total = total + shares[i].astype(F32)
    total = jnp.transpose(total)
    total = jnp.concatenate([total[:ROWS], total[ROWS:]], axis=1)[:, : tokens.shape[1]]
    mixed[...] = (tokens[...].astype(F32) + total).astype(BF)


def local(
    tokens, lengths, gain_attn, bias_attn, gain_mlp, bias_mlp, w_qkv, w_out, w_up, w_down, cache
):
    rows, narrow = tokens.shape
    wide = gain_attn.shape[0]

    mine = pl.pallas_call(
        hold_kernel,
        out_shape=pltpu.VMEM((rows, narrow), BF),
        in_specs=[pl.BlockSpec(memory_space=pl.ANY)],
        out_specs=VM,
        scratch_shapes=[pltpu.SemaphoreType.DMA],
        compiler_params=pltpu.CompilerParams(vmem_limit_bytes=1 << 20),
        cost_estimate=pl.CostEstimate(flops=20 << 30, bytes_accessed=96 << 20, transcendentals=0),
        name="hold",
    )(pltpu.with_memory_space_constraint(tokens, pltpu.HBM))
    pair = pl.pallas_call(
        pair_kernel,
        out_shape=jax.ShapeDtypeStruct((2, rows, narrow), BF),
        in_specs=[VM] * 2,
        out_specs=VM,
        compiler_params=pltpu.CompilerParams(vmem_limit_bytes=1 << 20),
        name="pair",
    )(in_vmem(mine), swap_core(tokens))
    got = [pair] + [shift_z(pair, k) for k in (1, 2, 3)]
    vectors = [v.reshape(1, wide) for v in (gain_mlp, bias_mlp, gain_attn, bias_attn)]
    held = vectors + [w_up, w_qkv]
    payload = pl.pallas_call(
        product_kernel,
        out_shape=jax.ShapeDtypeStruct((GY, PAYLOAD, BLOCK), BF),
        in_specs=[VM] * 10,
        out_specs=VM,
        scratch_shapes=[
            pltpu.VMEM((8, rows, narrow), BF),
            pltpu.VMEM((rows, wide), F32),
            pltpu.VMEM((2, rows * QKV_BLOCKS, LANES), F32),
            pltpu.VMEM((2 * QKV_BLOCKS, BLOCK), F32),
        ],
        compiler_params=PARAMS,
        name="product",
    )(*got, *[in_vmem(x) for x in held])

    steps = np.arange(HD // 2, dtype=np.float64) * (2.0 / HD)
    inverse = jnp.asarray(np.tile(np.power(THETA, -steps), 4)[None].astype(np.float32))
    summed = lax.all_to_all(payload, "gy", 0, 0)
    block, new_kv = pl.pallas_call(
        functools.partial(middle_kernel, wide),
        out_shape=(
            jax.ShapeDtypeStruct((RESULT, BLOCK), BF),
            jax.ShapeDtypeStruct((OWN, 2 * HD), BF),
        ),
        in_specs=[SM] + [VM] * 3,
        out_specs=(VM, VM),
        scratch_shapes=[pltpu.VMEM((LANES, LANES), F32)],
        compiler_params=PARAMS,
        name="middle",
    )(lengths, summed, inverse, in_vmem(cache))

    every = lax.all_to_all(jnp.broadcast_to(block[None], (GY, RESULT, BLOCK)), "gy", 0, 0)
    shares = pl.pallas_call(
        last_kernel,
        out_shape=jax.ShapeDtypeStruct((8, ROWS, LANES), BF),
        in_specs=[VM] * 3,
        out_specs=VM,
        scratch_shapes=[
            pltpu.VMEM((2, rows * QKV_BLOCKS, LANES), F32),
            pltpu.VMEM((2 * rows, w_down.shape[0] + 15 * LANES), BF),
            pltpu.VMEM((8 * narrow + 16, LANES), F32),
        ],
        compiler_params=PARAMS,
        name="last",
    )(every, in_vmem(w_down.T), in_vmem(w_out.T))

    mixed = pl.pallas_call(
        finish_kernel,
        out_shape=jax.ShapeDtypeStruct((rows, narrow), BF),
        in_specs=[VM] * 2,
        out_specs=VM,
        compiler_params=pltpu.CompilerParams(vmem_limit_bytes=1 << 20),
        name="finish",
    )(lax.all_to_all(shares, "gx", 0, 0), tokens)
    return (mixed, new_kv.reshape(OWN, 1, 2 * HD))


def solution(mesh):
    in_specs = (
        P(None, ("gy", "gx")),
        P("gy"),
        P("gy"),
        P("gy"),
        P("gy"),
        P("gy"),
        P("gy", "gx"),
        P("gx", "gy"),
        P("gy", "gx"),
        P("gx", "gy"),
        P("gy", "gx", None, None),
    )
    out_specs = (P(None, ("gy", "gx")), P("gy", "gx", None))
    return jax.shard_map(local, mesh=mesh, in_specs=in_specs, out_specs=out_specs, check_vma=False)
```

```python
import functools
import math

import jax
import jax.numpy as jnp
import numpy as np
from jax import lax
from jax.experimental import pallas as pl
from jax.experimental.pallas import tpu as pltpu
from jax.sharding import PartitionSpec as P

HD = 64
QPG = 29
EPS = 1e-05
THETA = 10000.0
BF = jnp.bfloat16
F32 = jnp.float32
LANES = 128
GY = 16
OWN = 4
ROWS = GY * OWN
BLOCK = 256
QKV_BLOCKS = 8
AT_SIDE = ROWS
AT_QKV = AT_SIDE + 8
AT_GAIN = AT_QKV + OWN * QKV_BLOCKS
AT_BIAS = AT_GAIN + QKV_BLOCKS
PAYLOAD = AT_BIAS + QKV_BLOCKS
RESULT = ROWS + OWN * QKV_BLOCKS
VM = pl.BlockSpec(memory_space=pltpu.VMEM)
PARAMS = pltpu.CompilerParams(vmem_limit_bytes=16 << 20)


def in_vmem(x):
    return pltpu.with_memory_space_constraint(x, pltpu.VMEM)


def hold_kernel(mine, out, sem):
    copy = pltpu.make_async_copy(mine, out, sem)
    copy.start()
    copy.wait()


def pair_kernel(mine, other, out):
    out[0] = mine[...]
    out[1] = other[...]


def swap_core(x):
    return lax.ppermute(x, "gx", [(i, i ^ 1) for i in range(8)])


def shift_z(x, k):
    return lax.ppermute(x, "gx", [(i, (i + 2 * k) % 8) for i in range(8)])


def chunks(total, step):
    return [(at, min(step, total - at)) for at in range(0, total, step)]


def three(value):
    out = []
    for _ in range(3):
        part = value.astype(BF).astype(F32)
        out.append(part)
        value = value - part
    return out


def product_kernel(g0, g1, g2, g3, gm, bm, ga, ba, w_up, w_qkv, out, blocks, flat, spread, side):
    at = lax.axis_index("gx")
    z, core = lax.div(at, 2), lax.rem(at, 2)
    narrow = g0.shape[2]
    wide = 8 * narrow
    for k, g in enumerate((g0, g1, g2, g3)):
        at = lax.rem(z + 4 - k, 4)
        blocks[2 * at + core] = g[0]
        blocks[2 * at + 1 - core] = g[1]
    for i in range(8):
        flat[:, narrow * i : narrow * (i + 1)] = blocks[i].astype(F32)
    values = flat[...]
    part_sum = jnp.sum(values, axis=1, keepdims=True)
    shifted = values - part_sum * (1.0 / wide)
    part_square = jnp.sum(shifted * shifted, axis=1, keepdims=True)
    up_cols, qkv_cols = w_up.shape[1], w_qkv.shape[1]

    lane = lax.broadcasted_iota(jnp.int32, (ROWS, LANES), 1)
    stats = jnp.zeros(lane.shape, F32)
    for i, part in enumerate(three(part_sum) + three(part_square)):
        stats = jnp.where(lane == 2 + i, part, stats)
    stats = jnp.transpose(stats)[:8]
    stats = jnp.concatenate([stats, jnp.zeros((8, BLOCK - ROWS), F32)], axis=1)
    row = lax.broadcasted_iota(jnp.int32, (8, 1), 0)

    def left(gain, bias):
        lower = jnp.where(row == 0, gain[...], jnp.where(row == 1, bias[...], 0.0))
        return jnp.concatenate([shifted * gain[...], lower], axis=0).astype(BF)

    left_m = left(gm, bm)
    for at, size in chunks(up_cols, 2 * BLOCK):
        got = jnp.dot(left_m, w_up[:, at : at + size], preferred_element_type=F32)
        if size < 2 * BLOCK:
            got = jnp.concatenate([got, jnp.zeros((ROWS + 8, 2 * BLOCK - size), F32)], axis=1)
        for j in range(2):
            p = at // BLOCK + j
            part = got[:, j * BLOCK : (j + 1) * BLOCK]
            out[p, :ROWS, :] = part[:ROWS].astype(BF)
            out[p, AT_SIDE:AT_QKV, :] = jnp.where(row < 2, part[ROWS:], stats).astype(BF)
    left_a = left(ga, ba)
    for at, size in chunks(qkv_cols, 2 * BLOCK):
        got = jnp.dot(left_a, w_qkv[:, at : at + size], preferred_element_type=F32)
        if size < 2 * BLOCK:
            got = jnp.concatenate([got, jnp.zeros((ROWS + 8, 2 * BLOCK - size), F32)], axis=1)
        for j in range(2):
            b = at // BLOCK + j
            part = got[:, j * BLOCK : (j + 1) * BLOCK]
            for h in range(2):
                cols = slice(h * LANES, (h + 1) * LANES)
                spread[h, pl.ds(b, ROWS, stride=QKV_BLOCKS), :] = part[:ROWS, cols]
            side[b : b + 1, :] = part[ROWS : ROWS + 1]
            side[QKV_BLOCKS + b : QKV_BLOCKS + b + 1, :] = part[ROWS + 1 : ROWS + 2]
    both = side[...].astype(BF)
    step = OWN * QKV_BLOCKS
    for p in range(GY):
        for h in range(2):
            cols = slice(h * LANES, (h + 1) * LANES)
            out[p, AT_QKV:AT_GAIN, cols] = spread[h, p * step : (p + 1) * step, :].astype(BF)
        out[p, AT_GAIN:, :] = both


def middle_kernel(wide, lengths, got, inverse, cache, block, new_kv, columns):
    width = wide * GY
    own_at = lax.axis_index("gy") * OWN

    sums, squares = [], []
    for d in range(GY):
        stat = got[d, AT_SIDE:AT_QKV, :LANES].astype(F32)
        sums.append(stat[2:3] + stat[3:4] + stat[4:5])
        squares.append(stat[5:6] + stat[6:7] + stat[7:8])
    mean = functools.reduce(jnp.add, sums) * (1.0 / width)
    gaps = [s * (1.0 / wide) - mean for s in sums]
    var = functools.reduce(jnp.add, [q + wide * g * g for q, g in zip(squares, gaps)]) * (1.0 / width)
    scale = 1.0 / jnp.sqrt(var + EPS)
    table = jnp.concatenate(gaps + [scale, jnp.zeros((LANES - GY - 1, LANES), F32)], axis=0)
    columns[...] = jnp.transpose(table)
    whole = columns[:ROWS]

    plain = jnp.zeros((QKV_BLOCKS, BLOCK), F32)
    for d in range(GY):
        plain = plain + got[d, AT_BIAS:, :].astype(F32)
    lane = lax.broadcasted_iota(jnp.int32, (1, LANES), 1)
    first = lane < HD
    half = lane % HD < HD // 2
    length = cache.shape[2]
    position = lax.broadcasted_iota(jnp.int32, (1, length), 1)
    factor = 1.0 / math.sqrt(HD)

    queries, keys_new, values_new = [], [], []
    for r in range(OWN):
        mine = columns[pl.ds(own_at + r, 1), :]
        acc = jnp.zeros((QKV_BLOCKS, BLOCK), F32)
        for d in range(GY):
            lo = AT_QKV + QKV_BLOCKS * r
            part = got[d, lo : lo + QKV_BLOCKS, :].astype(F32)
            acc = acc + (part + mine[:, d : d + 1] * got[d, AT_GAIN:AT_BIAS, :].astype(F32))
        qkv = (mine[:, GY : GY + 1] * acc + plain).astype(BF).astype(F32)
        angle = lengths[:, r : r + 1].astype(F32) * inverse[...]
        cosine = jnp.cos(angle)
        sine = jnp.sin(angle)
        sine = jnp.where(half, -sine, sine)
        pieces = []
        for h in range(2):
            pairs = qkv[:, h * LANES : (h + 1) * LANES]
            other = jnp.where(
                half, pltpu.roll(pairs, LANES - HD // 2, 1), pltpu.roll(pairs, HD // 2, 1)
            )
            turned = (pairs * cosine + other * sine).astype(BF).astype(F32)
            pieces.append(jnp.where(first, turned, 0.0))
            pieces.append(jnp.where(first, pltpu.roll(turned, HD, 1), 0.0))
        query = jnp.concatenate(pieces, axis=0)
        key = query[15:16]
        value = jnp.where(first, 0.0, pltpu.roll(qkv[7:8, LANES:], HD, 1))
        new_kv[r : r + 1, :] = (key + value).astype(BF)
        queries.append(query * factor)
        keys_new.append(key)
        values_new.append(value)

    def score(r):
        scores = lax.dot_general(
            queries[r].astype(BF), cache[r, 0], (((1,), (1,)), ((), ())), preferred_element_type=F32
        )
        return jnp.where(position < lengths[:, r : r + 1], scores, -jnp.inf)

    def soften(r, scores):
        own = jnp.sum(queries[r] * keys_new[r], axis=1, keepdims=True)
        top = jnp.maximum(jnp.max(scores, axis=1, keepdims=True), own)
        probs = jnp.exp(scores - top)
        own_prob = jnp.exp(own - top)
        total = jnp.sum(probs, axis=1, keepdims=True) + own_prob
        return probs.astype(BF), own_prob, total

    def mix(r, probs, own_prob, total):
        summed = jnp.dot(probs, cache[r, 0], preferred_element_type=F32)
        summed = summed + own_prob.astype(BF).astype(F32) * values_new[r]
        result = summed / total
        lo = ROWS + QKV_BLOCKS * r
        for h in range(2):
            even, odd = result[16 * h : 16 * h + 8], result[16 * h + 8 : 16 * h + 16]
            pairs = jnp.where(first, pltpu.roll(even, HD, 1), odd)
            block[lo : lo + QKV_BLOCKS, h * LANES : (h + 1) * LANES] = pairs.astype(BF)

    soft = {}
    scores = score(0)
    for r in range(OWN):
        following = score(r + 1) if r + 1 < OWN else None
        soft[r] = soften(r, scores)
        if r > 0:
            mix(r - 1, *soft.pop(r - 1))
        scores = following

    acc = jnp.zeros((ROWS, BLOCK), F32)
    plain = jnp.zeros((1, BLOCK), F32)
    for d in range(GY):
        side = got[d, AT_SIDE:AT_QKV, :].astype(F32)
        acc = acc + (got[d, :ROWS, :].astype(F32) + whole[:, d : d + 1] * side[0:1])
        plain = plain + side[1:2]
    up = whole[:, GY : GY + 1] * acc + plain
    hidden = 0.5 * up * (1.0 + lax.erf(up * math.sqrt(0.5)))
    block[:ROWS, :] = hidden.astype(BF)
    mix(OWN - 1, *soft.pop(OWN - 1))


def last_kernel(every, w_down, w_out, out, spread, left, turned):
    up_cols, attn_cols = w_down.shape[1], w_out.shape[1]
    narrow = w_down.shape[0] // 8
    step = OWN * QKV_BLOCKS
    for d in range(GY):
        for h in range(2):
            cols = slice(h * LANES, (h + 1) * LANES)
            spread[h, d * step : (d + 1) * step, :] = every[d, ROWS:, cols].astype(F32)
    for d, (at, size) in enumerate(chunks(up_cols, BLOCK)):
        part = every[d, :ROWS, :size]
        left[:ROWS, at : at + size] = part
        left[ROWS:, at : at + size] = part
    for t in range(-(-attn_cols // LANES)):
        part = spread[t % 2, pl.ds(t // 2, ROWS, stride=QKV_BLOCKS), :].astype(BF)
        at = up_cols + t * LANES
        left[:ROWS, at : at + LANES] = part
        left[ROWS:, at : at + LANES] = part
    both = (((1,), (1,)), ((), ()))
    total = lax.dot_general(w_down[...], left[:, :up_cols], both, preferred_element_type=F32)
    total = total + lax.dot_general(
        w_out[...], left[:, up_cols : up_cols + attn_cols], both, preferred_element_type=F32
    )
    turned[: 8 * narrow, :] = total
    turned[8 * narrow :, :] = jnp.zeros((turned.shape[0] - 8 * narrow, LANES), F32)
    first = lax.broadcasted_iota(jnp.int32, (1, LANES), 1) < ROWS
    for i in range(8):
        at = narrow * i
        upper, lower = turned[at : at + ROWS, :], turned[at + ROWS : at + 2 * ROWS, :]
        out[i] = jnp.where(first, upper, lower).astype(BF)


def finish_kernel(shares, tokens, held_kv, mixed, new_kv):
    new_kv[...] = held_kv[...]
    total = shares[0].astype(F32)
    for i in range(1, 8):
        total = total + shares[i].astype(F32)
    total = jnp.transpose(total)
    total = jnp.concatenate([total[:ROWS], total[ROWS:]], axis=1)[:, : tokens.shape[1]]
    mixed[...] = (tokens[...].astype(F32) + total).astype(BF)


def local(
    tokens, lengths, gain_attn, bias_attn, gain_mlp, bias_mlp, w_qkv, w_out, w_up, w_down, cache
):
    rows, narrow = tokens.shape
    wide = gain_attn.shape[0]

    mine = pl.pallas_call(
        hold_kernel,
        out_shape=pltpu.VMEM((rows, narrow), BF),
        in_specs=[pl.BlockSpec(memory_space=pl.ANY)],
        out_specs=VM,
        scratch_shapes=[pltpu.SemaphoreType.DMA],
        compiler_params=pltpu.CompilerParams(vmem_limit_bytes=1 << 20),
        cost_estimate=pl.CostEstimate(flops=20 << 30, bytes_accessed=96 << 20, transcendentals=0),
        name="hold",
    )(pltpu.with_memory_space_constraint(tokens, pltpu.HBM))
    pair = pl.pallas_call(
        pair_kernel,
        out_shape=jax.ShapeDtypeStruct((2, rows, narrow), BF),
        in_specs=[VM] * 2,
        out_specs=VM,
        compiler_params=pltpu.CompilerParams(vmem_limit_bytes=1 << 20),
        name="pair",
    )(in_vmem(mine), swap_core(tokens))
    got = [pair] + [shift_z(pair, k) for k in (1, 2, 3)]
    vectors = [v.reshape(1, wide) for v in (gain_mlp, bias_mlp, gain_attn, bias_attn)]
    held = vectors + [w_up, w_qkv]
    payload = pl.pallas_call(
        product_kernel,
        out_shape=jax.ShapeDtypeStruct((GY, PAYLOAD, BLOCK), BF),
        in_specs=[VM] * 10,
        out_specs=VM,
        scratch_shapes=[
            pltpu.VMEM((8, rows, narrow), BF),
            pltpu.VMEM((rows, wide), F32),
            pltpu.VMEM((2, rows * QKV_BLOCKS, LANES), F32),
            pltpu.VMEM((2 * QKV_BLOCKS, BLOCK), F32),
        ],
        compiler_params=PARAMS,
        name="product",
    )(*got, *[in_vmem(x) for x in held])

    steps = np.arange(HD // 2, dtype=np.float64) * (2.0 / HD)
    inverse = jnp.asarray(np.tile(np.power(THETA, -steps), 4)[None].astype(np.float32))
    summed = lax.all_to_all(payload, "gy", 0, 0)
    block, new_kv = pl.pallas_call(
        functools.partial(middle_kernel, wide),
        out_shape=(
            jax.ShapeDtypeStruct((RESULT, BLOCK), BF),
            pltpu.VMEM((OWN, 2 * HD), BF),
        ),
        in_specs=[VM] * 4,
        out_specs=(VM, VM),
        scratch_shapes=[pltpu.VMEM((LANES, LANES), F32)],
        compiler_params=PARAMS,
        name="middle",
    )(lengths.reshape(1, OWN), summed, inverse, in_vmem(cache))

    every = lax.all_to_all(jnp.broadcast_to(block[None], (GY, RESULT, BLOCK)), "gy", 0, 0)
    shares = pl.pallas_call(
        last_kernel,
        out_shape=jax.ShapeDtypeStruct((8, ROWS, LANES), BF),
        in_specs=[VM] * 3,
        out_specs=VM,
        scratch_shapes=[
            pltpu.VMEM((2, rows * QKV_BLOCKS, LANES), F32),
            pltpu.VMEM((2 * rows, w_down.shape[0] + 15 * LANES), BF),
            pltpu.VMEM((8 * narrow + 16, LANES), F32),
        ],
        compiler_params=PARAMS,
        name="last",
    )(every, in_vmem(w_down.T), in_vmem(w_out.T))

    mixed, new_kv = pl.pallas_call(
        finish_kernel,
        out_shape=(
            jax.ShapeDtypeStruct((rows, narrow), BF),
            jax.ShapeDtypeStruct((OWN, 2 * HD), BF),
        ),
        in_specs=[VM] * 3,
        out_specs=(VM, VM),
        compiler_params=pltpu.CompilerParams(vmem_limit_bytes=1 << 20),
        name="finish",
    )(lax.all_to_all(shares, "gx", 0, 0), in_vmem(mine), in_vmem(new_kv))
    return (mixed, new_kv.reshape(OWN, 1, 2 * HD))


def solution(mesh):
    in_specs = (
        P(None, ("gy", "gx")),
        P("gy"),
        P("gy"),
        P("gy"),
        P("gy"),
        P("gy"),
        P("gy", "gx"),
        P("gx", "gy"),
        P("gy", "gx"),
        P("gx", "gy"),
        P("gy", "gx", None, None),
    )
    out_specs = (P(None, ("gy", "gx")), P("gy", "gx", None))
    return jax.shard_map(local, mesh=mesh, in_specs=in_specs, out_specs=out_specs, check_vma=False)
```

```python
import functools
import math

import jax
import jax.numpy as jnp
import numpy as np
from jax import lax
from jax.experimental import pallas as pl
from jax.experimental.pallas import tpu as pltpu
from jax.sharding import PartitionSpec as P

HD = 64
QPG = 29
EPS = 1e-05
THETA = 10000.0
BF = jnp.bfloat16
F32 = jnp.float32
LANES = 128
GY = 16
OWN = 4
ROWS = GY * OWN
BLOCK = 256
QKV_BLOCKS = 8
AT_SIDE = ROWS
AT_QKV = AT_SIDE + 8
AT_GAIN = AT_QKV + OWN * QKV_BLOCKS
AT_BIAS = AT_GAIN + QKV_BLOCKS
PAYLOAD = AT_BIAS + QKV_BLOCKS
RESULT = ROWS + OWN * QKV_BLOCKS
VM = pl.BlockSpec(memory_space=pltpu.VMEM)
PARAMS = pltpu.CompilerParams(vmem_limit_bytes=16 << 20)


def in_vmem(x):
    return pltpu.with_memory_space_constraint(x, pltpu.VMEM)


def hold_kernel(mine, out, sem):
    copy = pltpu.make_async_copy(mine, out, sem)
    copy.start()
    copy.wait()


def pair_kernel(mine, other, out):
    out[0] = mine[...]
    out[1] = other[...]


def swap_core(x):
    return lax.ppermute(x, "gx", [(i, i ^ 1) for i in range(8)])


def shift_z(x, k):
    return lax.ppermute(x, "gx", [(i, (i + 2 * k) % 8) for i in range(8)])


def chunks(total, step):
    return [(at, min(step, total - at)) for at in range(0, total, step)]


def three(value):
    out = []
    for _ in range(3):
        part = value.astype(BF).astype(F32)
        out.append(part)
        value = value - part
    return out


def product_kernel(g0, g1, g2, g3, gm, bm, ga, ba, w_up, w_qkv, out, blocks, flat, spread, side):
    at = lax.axis_index("gx")
    z, core = lax.div(at, 2), lax.rem(at, 2)
    narrow = g0.shape[2]
    wide = 8 * narrow
    for k, g in enumerate((g0, g1, g2, g3)):
        at = lax.rem(z + 4 - k, 4)
        blocks[2 * at + core] = g[0]
        blocks[2 * at + 1 - core] = g[1]
    for i in range(8):
        flat[:, narrow * i : narrow * (i + 1)] = blocks[i].astype(F32)
    values = flat[...]
    part_sum = jnp.sum(values, axis=1, keepdims=True)
    shifted = values - part_sum * (1.0 / wide)
    part_square = jnp.sum(shifted * shifted, axis=1, keepdims=True)
    up_cols, qkv_cols = w_up.shape[1], w_qkv.shape[1]

    lane = lax.broadcasted_iota(jnp.int32, (ROWS, LANES), 1)
    stats = jnp.zeros(lane.shape, F32)
    for i, part in enumerate(three(part_sum) + three(part_square)):
        stats = jnp.where(lane == 2 + i, part, stats)
    stats = jnp.transpose(stats)[:8]
    stats = jnp.concatenate([stats, jnp.zeros((8, BLOCK - ROWS), F32)], axis=1)
    row = lax.broadcasted_iota(jnp.int32, (8, 1), 0)

    def left(gain, bias):
        lower = jnp.where(row == 0, gain[...], jnp.where(row == 1, bias[...], 0.0))
        return jnp.concatenate([shifted * gain[...], lower], axis=0).astype(BF)

    left_m = left(gm, bm)
    for at, size in chunks(up_cols, 2 * BLOCK):
        got = jnp.dot(left_m, w_up[:, at : at + size], preferred_element_type=F32)
        if size < 2 * BLOCK:
            got = jnp.concatenate([got, jnp.zeros((ROWS + 8, 2 * BLOCK - size), F32)], axis=1)
        for j in range(2):
            p = at // BLOCK + j
            part = got[:, j * BLOCK : (j + 1) * BLOCK]
            out[p, :ROWS, :] = part[:ROWS].astype(BF)
            out[p, AT_SIDE:AT_QKV, :] = jnp.where(row < 2, part[ROWS:], stats).astype(BF)
    left_a = left(ga, ba)
    for at, size in chunks(qkv_cols, 2 * BLOCK):
        got = jnp.dot(left_a, w_qkv[:, at : at + size], preferred_element_type=F32)
        if size < 2 * BLOCK:
            got = jnp.concatenate([got, jnp.zeros((ROWS + 8, 2 * BLOCK - size), F32)], axis=1)
        for j in range(2):
            b = at // BLOCK + j
            part = got[:, j * BLOCK : (j + 1) * BLOCK]
            for h in range(2):
                cols = slice(h * LANES, (h + 1) * LANES)
                spread[h, pl.ds(b, ROWS, stride=QKV_BLOCKS), :] = part[:ROWS, cols]
            side[b : b + 1, :] = part[ROWS : ROWS + 1]
            side[QKV_BLOCKS + b : QKV_BLOCKS + b + 1, :] = part[ROWS + 1 : ROWS + 2]
    both = side[...].astype(BF)
    step = OWN * QKV_BLOCKS
    for p in range(GY):
        for h in range(2):
            cols = slice(h * LANES, (h + 1) * LANES)
            out[p, AT_QKV:AT_GAIN, cols] = spread[h, p * step : (p + 1) * step, :].astype(BF)
        out[p, AT_GAIN:, :] = both


def middle_kernel(wide, lengths, got, inverse, cache, block, new_kv, columns):
    width = wide * GY
    own_at = lax.axis_index("gy") * OWN

    sums, squares = [], []
    for d in range(GY):
        stat = got[d, AT_SIDE:AT_QKV, :LANES].astype(F32)
        sums.append(stat[2:3] + stat[3:4] + stat[4:5])
        squares.append(stat[5:6] + stat[6:7] + stat[7:8])
    mean = functools.reduce(jnp.add, sums) * (1.0 / width)
    gaps = [s * (1.0 / wide) - mean for s in sums]
    var = functools.reduce(jnp.add, [q + wide * g * g for q, g in zip(squares, gaps)]) * (1.0 / width)
    scale = 1.0 / jnp.sqrt(var + EPS)
    table = jnp.concatenate(gaps + [scale, jnp.zeros((LANES - GY - 1, LANES), F32)], axis=0)
    columns[...] = jnp.transpose(table)
    whole = columns[:ROWS]

    plain = jnp.zeros((QKV_BLOCKS, BLOCK), F32)
    for d in range(GY):
        plain = plain + got[d, AT_BIAS:, :].astype(F32)
    lane = lax.broadcasted_iota(jnp.int32, (1, LANES), 1)
    first = lane < HD
    half = lane % HD < HD // 2
    length = cache.shape[2]
    position = lax.broadcasted_iota(jnp.int32, (1, length), 1)
    factor = 1.0 / math.sqrt(HD)

    queries, keys_new, values_new = [], [], []
    for r in range(OWN):
        mine = columns[pl.ds(own_at + r, 1), :]
        acc = jnp.zeros((QKV_BLOCKS, BLOCK), F32)
        for d in range(GY):
            lo = AT_QKV + QKV_BLOCKS * r
            part = got[d, lo : lo + QKV_BLOCKS, :].astype(F32)
            acc = acc + (part + mine[:, d : d + 1] * got[d, AT_GAIN:AT_BIAS, :].astype(F32))
        qkv = (mine[:, GY : GY + 1] * acc + plain).astype(BF).astype(F32)
        angle = lengths[:, r : r + 1].astype(F32) * inverse[...]
        cosine = jnp.cos(angle)
        sine = jnp.sin(angle)
        sine = jnp.where(half, -sine, sine)
        pieces = []
        for h in range(2):
            pairs = qkv[:, h * LANES : (h + 1) * LANES]
            other = jnp.where(
                half, pltpu.roll(pairs, LANES - HD // 2, 1), pltpu.roll(pairs, HD // 2, 1)
            )
            turned = (pairs * cosine + other * sine).astype(BF).astype(F32)
            pieces.append(jnp.where(first, turned, 0.0))
            pieces.append(jnp.where(first, pltpu.roll(turned, HD, 1), 0.0))
        query = jnp.concatenate(pieces, axis=0)
        key = query[15:16]
        value = jnp.where(first, 0.0, pltpu.roll(qkv[7:8, LANES:], HD, 1))
        new_kv[r : r + 1, :] = (key + value).astype(BF)
        queries.append(query * factor)
        keys_new.append(key)
        values_new.append(value)

    def score(r):
        scores = lax.dot_general(
            queries[r].astype(BF), cache[r, 0], (((1,), (1,)), ((), ())), preferred_element_type=F32
        )
        return jnp.where(position < lengths[:, r : r + 1], scores, -jnp.inf)

    def soften(r, scores):
        own = jnp.sum(queries[r] * keys_new[r], axis=1, keepdims=True)
        top = jnp.maximum(jnp.max(scores, axis=1, keepdims=True), own)
        probs = jnp.exp(scores - top)
        own_prob = jnp.exp(own - top)
        total = jnp.sum(probs, axis=1, keepdims=True) + own_prob
        return probs.astype(BF), own_prob, total

    def mix(r, probs, own_prob, total):
        summed = jnp.dot(probs, cache[r, 0], preferred_element_type=F32)
        summed = summed + own_prob.astype(BF).astype(F32) * values_new[r]
        result = summed / total
        lo = ROWS + QKV_BLOCKS * r
        for h in range(2):
            even, odd = result[16 * h : 16 * h + 8], result[16 * h + 8 : 16 * h + 16]
            pairs = jnp.where(first, pltpu.roll(even, HD, 1), odd)
            block[lo : lo + QKV_BLOCKS, h * LANES : (h + 1) * LANES] = pairs.astype(BF)

    soft = {}
    scores = score(0)
    for r in range(OWN):
        following = score(r + 1) if r + 1 < OWN else None
        soft[r] = soften(r, scores)
        if r > 0:
            mix(r - 1, *soft.pop(r - 1))
        scores = following

    acc = jnp.zeros((ROWS, BLOCK), F32)
    plain = jnp.zeros((1, BLOCK), F32)
    for d in range(GY):
        side = got[d, AT_SIDE:AT_QKV, :].astype(F32)
        acc = acc + (got[d, :ROWS, :].astype(F32) + whole[:, d : d + 1] * side[0:1])
        plain = plain + side[1:2]
    up = whole[:, GY : GY + 1] * acc + plain
    hidden = 0.5 * up * (1.0 + lax.erf(up * math.sqrt(0.5)))
    block[:ROWS, :] = hidden.astype(BF)
    mix(OWN - 1, *soft.pop(OWN - 1))


def last_kernel(every, w_down, w_out, out, spread, left, turned):
    up_cols, attn_cols = w_down.shape[1], w_out.shape[1]
    narrow = w_down.shape[0] // 8
    step = OWN * QKV_BLOCKS
    for d in range(GY):
        for h in range(2):
            cols = slice(h * LANES, (h + 1) * LANES)
            spread[h, d * step : (d + 1) * step, :] = every[d, ROWS:, cols].astype(F32)
    both = (((1,), (1,)), ((), ()))
    total = None
    for d, (at, size) in enumerate(chunks(up_cols, BLOCK)):
        part = every[d, :ROWS, :size]
        part = jnp.concatenate([part, part], axis=0)
        one = lax.dot_general(w_down[:, at : at + size], part, both, preferred_element_type=F32)
        total = one if total is None else total + one
    for t, (at, size) in enumerate(chunks(attn_cols, LANES)):
        part = spread[t % 2, pl.ds(t // 2, ROWS, stride=QKV_BLOCKS), :].astype(BF)
        left[:ROWS, at : at + LANES] = part
        left[ROWS:, at : at + LANES] = part
    total = total + lax.dot_general(
        w_out[...], left[:, :attn_cols], both, preferred_element_type=F32
    )
    turned[: 8 * narrow, :] = total
    turned[8 * narrow :, :] = jnp.zeros((turned.shape[0] - 8 * narrow, LANES), F32)
    first = lax.broadcasted_iota(jnp.int32, (1, LANES), 1) < ROWS
    for i in range(8):
        at = narrow * i
        upper, lower = turned[at : at + ROWS, :], turned[at + ROWS : at + 2 * ROWS, :]
        out[i] = jnp.where(first, upper, lower).astype(BF)


def finish_kernel(shares, tokens, held_kv, mixed, new_kv):
    new_kv[...] = held_kv[...]
    total = shares[0].astype(F32)
    for i in range(1, 8):
        total = total + shares[i].astype(F32)
    total = jnp.transpose(total)
    total = jnp.concatenate([total[:ROWS], total[ROWS:]], axis=1)[:, : tokens.shape[1]]
    mixed[...] = (tokens[...].astype(F32) + total).astype(BF)


def local(
    tokens, lengths, gain_attn, bias_attn, gain_mlp, bias_mlp, w_qkv, w_out, w_up, w_down, cache
):
    rows, narrow = tokens.shape
    wide = gain_attn.shape[0]

    mine = pl.pallas_call(
        hold_kernel,
        out_shape=pltpu.VMEM((rows, narrow), BF),
        in_specs=[pl.BlockSpec(memory_space=pl.ANY)],
        out_specs=VM,
        scratch_shapes=[pltpu.SemaphoreType.DMA],
        compiler_params=pltpu.CompilerParams(vmem_limit_bytes=1 << 20),
        cost_estimate=pl.CostEstimate(flops=20 << 30, bytes_accessed=96 << 20, transcendentals=0),
        name="hold",
    )(pltpu.with_memory_space_constraint(tokens, pltpu.HBM))
    pair = pl.pallas_call(
        pair_kernel,
        out_shape=jax.ShapeDtypeStruct((2, rows, narrow), BF),
        in_specs=[VM] * 2,
        out_specs=VM,
        compiler_params=pltpu.CompilerParams(vmem_limit_bytes=1 << 20),
        name="pair",
    )(in_vmem(mine), swap_core(tokens))
    got = [pair] + [shift_z(pair, k) for k in (1, 2, 3)]
    vectors = [v.reshape(1, wide) for v in (gain_mlp, bias_mlp, gain_attn, bias_attn)]
    held = vectors + [w_up, w_qkv]
    payload = pl.pallas_call(
        product_kernel,
        out_shape=jax.ShapeDtypeStruct((GY, PAYLOAD, BLOCK), BF),
        in_specs=[VM] * 10,
        out_specs=VM,
        scratch_shapes=[
            pltpu.VMEM((8, rows, narrow), BF),
            pltpu.VMEM((rows, wide), F32),
            pltpu.VMEM((2, rows * QKV_BLOCKS, LANES), F32),
            pltpu.VMEM((2 * QKV_BLOCKS, BLOCK), F32),
        ],
        compiler_params=PARAMS,
        name="product",
    )(*got, *[in_vmem(x) for x in held])

    steps = np.arange(HD // 2, dtype=np.float64) * (2.0 / HD)
    inverse = jnp.asarray(np.tile(np.power(THETA, -steps), 4)[None].astype(np.float32))
    summed = lax.all_to_all(payload, "gy", 0, 0)
    block, new_kv = pl.pallas_call(
        functools.partial(middle_kernel, wide),
        out_shape=(
            jax.ShapeDtypeStruct((RESULT, BLOCK), BF),
            pltpu.VMEM((OWN, 2 * HD), BF),
        ),
        in_specs=[VM] * 4,
        out_specs=(VM, VM),
        scratch_shapes=[pltpu.VMEM((LANES, LANES), F32)],
        compiler_params=PARAMS,
        name="middle",
    )(lengths.reshape(1, OWN), summed, inverse, in_vmem(cache))

    every = lax.all_to_all(jnp.broadcast_to(block[None], (GY, RESULT, BLOCK)), "gy", 0, 0)
    shares = pl.pallas_call(
        last_kernel,
        out_shape=jax.ShapeDtypeStruct((8, ROWS, LANES), BF),
        in_specs=[VM] * 3,
        out_specs=VM,
        scratch_shapes=[
            pltpu.VMEM((2, rows * QKV_BLOCKS, LANES), F32),
            pltpu.VMEM((2 * rows, 15 * LANES), BF),
            pltpu.VMEM((8 * narrow + 16, LANES), F32),
        ],
        compiler_params=PARAMS,
        name="last",
    )(every, in_vmem(w_down.T), in_vmem(w_out.T))

    mixed, new_kv = pl.pallas_call(
        finish_kernel,
        out_shape=(
            jax.ShapeDtypeStruct((rows, narrow), BF),
            jax.ShapeDtypeStruct((OWN, 2 * HD), BF),
        ),
        in_specs=[VM] * 3,
        out_specs=(VM, VM),
        compiler_params=pltpu.CompilerParams(vmem_limit_bytes=1 << 20),
        name="finish",
    )(lax.all_to_all(shares, "gx", 0, 0), in_vmem(mine), in_vmem(new_kv))
    return (mixed, new_kv.reshape(OWN, 1, 2 * HD))


def solution(mesh):
    in_specs = (
        P(None, ("gy", "gx")),
        P("gy"),
        P("gy"),
        P("gy"),
        P("gy"),
        P("gy"),
        P("gy", "gx"),
        P("gx", "gy"),
        P("gy", "gx"),
        P("gx", "gy"),
        P("gy", "gx", None, None),
    )
    out_specs = (P(None, ("gy", "gx")), P("gy", "gx", None))
    return jax.shard_map(local, mesh=mesh, in_specs=in_specs, out_specs=out_specs, check_vma=False)
```
